512 devices in a mesh: group: 8 (over x_hi, y), fsdp: 64 (over x_lo, z, core).
Axes of the slice: x: 4 (x_hi: 2, x_lo: 2; x = x_hi * 2 + x_lo), y: 4, z: 16, core: 2. Of those that a mesh axis runs over, the one named last changes fastest.
Arguments:
- gossip_step: int32 [1], replicated, may hold values from 0 to 199
- context: bfloat16 [8, 24576, 256], P('group', 'fsdp'), may hold values from -6 to 6
- upstream: bfloat16 [8, 24576, 4096], P('group', 'fsdp'), may hold values from -3 to 3
- master: float32 [8, 8192, 128], P('group', 'fsdp'), may hold values from -0.375 to 0.375
- moment_one: float32 [8, 8192, 128], P('group', 'fsdp'), may hold values from -3 to 3
- moment_two: float32 [8, 8192, 128], P('group', 'fsdp'), may hold values from 0.0001 to 0.01
Outputs:
- context_grad: bfloat16 [8, 24576, 256], P('group', 'fsdp')
- master_out: float32 [8, 8192, 128], P('group', 'fsdp')
- moment_one_out: float32 [8, 8192, 128], P('group', 'fsdp')
- moment_two_out: float32 [8, 8192, 128], P('group', 'fsdp')
The draws below stay inside these ranges and needn't reach their ends.
All inputs are finite; a program needn't handle non-finite values.
Results may differ from the reference program's by a relative error of at most 0.0049.
Values may be sent and summed in bfloat16 or wider, within the bound.
A program may use at most 64 MiB of HBM per device.

```python
import math
import jax
import jax.numpy as jnp
from jax import lax

D = 4096
ROWS = 256
FLAT = 8192
TOKENS = 24576
GROUPS = 8
N_GROUP = 8


def shard_levels(key, extent, split, low, high):
    def one(position, blocks):
        draws = jax.random.uniform(jax.random.fold_in(jax.random.fold_in(key, 6), position), (blocks,), jnp.float32, low / len(split), high / len(split))
        return jnp.repeat(jnp.exp(draws), extent[position] // blocks).reshape((-1,) + (1,) * (len(extent) - position - 1))

    loudness = one(*split[0])
    for cut in split[1:]:
        loudness = loudness * one(*cut)
    return loudness


def scatter_about(rng, shape, scale, limit, split=(), kind=jnp.bfloat16):
    entries = jax.random.normal(rng, shape, jnp.float32) * scale
    if len(split) > 0:
        entries = shard_levels(rng, shape, split, -0.22, 0.18) * entries
    return jnp.clip(entries, min=-limit, max=limit).astype(kind)


def setup_inputs(seed: int = 0) -> dict:
    key_list = jax.random.split(jax.random.key(seed), 7)
    return {
        "gossip_step": jax.random.randint(key_list[0], (1,), 0, 200).astype(jnp.int32),
        "context": scatter_about(key_list[1], (GROUPS, TOKENS, ROWS), 1.0, 6.0, ((0, 8), (1, 64))),
        "upstream": scatter_about(key_list[2], (GROUPS, TOKENS, D), 0.5, 3.0, ((0, 8), (1, 64))),
        "master": scatter_about(key_list[3], (GROUPS, FLAT, 128), ROWS ** -0.5, 0.375, ((0, 8), (1, 64)), jnp.float32),
        "moment_one": scatter_about(key_list[4], (GROUPS, FLAT, 128), 0.5, 3.0, ((0, 8), (1, 64)), jnp.float32),
        "moment_two": jnp.clip(jnp.exp(math.log(0.01) - 4.6051702 * jax.random.uniform(key_list[5], (GROUPS, FLAT, 128), jnp.float32) ** shard_levels(key_list[5], (GROUPS, FLAT, 128), ((0, 8), (1, 64)), -0.2, 0.2)), 0.0001, 0.01),
    }


beta_one = 0.9
beta_two = 0.999
adam_eps = 1e-08
learn_rate = 0.003
decay_rate = 0.1

def reference(gossip_step, context, upstream, master, moment_one, moment_two):
    scale = 1.0 / math.sqrt(TOKENS)

    def one_group(items):
        group_context, group_upstream, group_master = items
        weight = group_master.astype(jnp.bfloat16).reshape(ROWS, D)
        context_grad = jnp.dot(group_upstream, weight.T, preferred_element_type=jnp.float32).astype(jnp.bfloat16)
        product = jnp.dot(group_context.T, group_upstream, preferred_element_type=jnp.float32)
        return (context_grad, product.reshape(FLAT, 128))
    context_grad, product = lax.map(one_group, (context, upstream, master))
    gradient = product * scale
    step_number = (gossip_step[0] + 1).astype(jnp.float32)
    first_moment = beta_one * moment_one + (1.0 - beta_one) * gradient
    second_moment = beta_two * moment_two + (1.0 - beta_two) * gradient * gradient
    fix_one = 1.0 - jnp.power(jnp.float32(beta_one), step_number)
    fix_two = 1.0 - jnp.power(jnp.float32(beta_two), step_number)
    update = first_moment / fix_one / (jnp.sqrt(second_moment / fix_two) + adam_eps)
    stepped = master - learn_rate * (update + decay_rate * master)
    bit_count = N_GROUP.bit_length() - 1
    chosen = gossip_step[0] % bit_count
    partners = jnp.bitwise_xor(jnp.arange(N_GROUP, dtype=jnp.int32), jnp.left_shift(jnp.int32(1), chosen))
    master_out = 0.5 * (stepped + stepped[partners])
    return (context_grad, master_out, first_moment, second_moment)
```

```python
import functools
import math

import jax
import jax.numpy as jnp
from jax import lax
from jax.experimental import pallas as pl
from jax.experimental.pallas import tpu as pltpu
from jax.sharding import PartitionSpec as P

MESH = pl.DeviceIdType.MESH
BF16 = jnp.bfloat16
F32 = jnp.float32

beta_one = 0.9
beta_two = 0.999
adam_eps = 1e-08
learn_rate = 0.003
decay_rate = 0.1

OWN = 4
PARTS = 4
REACH = 2
PIECE = 4


def power_of(base, count):
    total = jnp.full(count.shape, 1.0, F32)
    for bit in range(8):
        factor = jnp.float32(base ** (2**bit))
        total = jnp.where(((count >> bit) & 1) == 1, total * factor, total)
    return total


def kernel(
    NG, Z, tokens_all,
    step_ref, ctx_hbm, up_hbm, master_hbm, one_hbm, two_hbm,
    grad_hbm, master_out_hbm, one_out_hbm, two_out_hbm,
    ctx, up, master, one, two,
    gsum, own, csend, crecv, xsend, xrecv, zsend, zrecv,
    wbuf, wmat, cg, folded, stepped, sent, got,
    grad_out, master_out, one_out, two_out,
    in_sem, out_sem,
    azs, azr, axs, axr, acs, acr,
    rcs, rcr, rxs, rxr, rzs, rzr, gs, gr,
):
    T, D = up.shape
    Q = D // PARTS
    KK = Q // 128
    half = Z // 2
    bits = NG.bit_length() - 1
    group = lax.axis_index("group")
    index = lax.axis_index("fsdp")
    x = index // (2 * Z)
    z = lax.rem(index // 2, Z)
    c = lax.rem(index, 2)

    def at(x_, z_, c_):
        return (group, x_ * (2 * Z) + z_ * 2 + c_)

    def along(k):
        return at(x, lax.rem(z + (k + 2 * Z), Z), c)

    over = at(1 - x, z, c)
    beside = at(x, z, 1 - c)
    partners = [(jnp.bitwise_xor(group, 1 << b), index) for b in range(bits)]

    loads = {}

    def load(name, src, dst, n):
        copy = pltpu.make_async_copy(src, dst, in_sem.at[n])
        copy.start()
        loads[name] = copy

    load("master", master_hbm, master, 0)
    load("ctx", ctx_hbm, ctx, 1)
    for q in range(PARTS):
        load(("up", q), up_hbm.at[:, pl.ds(q * Q, Q)], up.at[:, pl.ds(q * Q, Q)], 2 + q)
    load("one", one_hbm, one, 2 + PARTS)
    load("two", two_hbm, two, 3 + PARTS)

    reach = min(REACH, half)
    hops = sorted({h % Z for h in range(1, reach + 1)} | {-h % Z for h in range(1, reach + 1)})
    peers = [along(h) for h in hops] + [over, beside] + partners
    barrier = pltpu.get_barrier_semaphore()
    for peer in peers:
        pl.semaphore_signal(barrier, inc=1, device_id=peer, device_id_type=MESH)

    started = []

    def send(copy):
        copy.start()
        started.append(copy)

    def remote(src, dst, ss, rs, to):
        return pltpu.make_async_remote_copy(
            src_ref=src, dst_ref=dst, send_sem=ss, recv_sem=rs, device_id=to, device_id_type=MESH
        )

    row8 = lax.broadcasted_iota(jnp.int32, (8, Q), 0)
    low = row8 < OWN

    def turn(value):
        return pltpu.roll(value, 4, 0)

    def z_of(k):
        return lax.rem(z + (2 * Z - k), Z)

    def a_z(k, hop):
        chunk = wbuf.at[x, c, z_of(k - hop)]
        there = k % Z
        return remote(chunk, chunk, azs.at[there], azr.at[there], along(hop))

    def a_x(k):
        chunk = wbuf.at[x, c, z_of(k)]
        return remote(chunk, chunk, axs.at[k % Z], axr.at[k % Z], over)

    def a_c(w, k):
        chunk = wbuf.at[x if w == 0 else 1 - x, c, z_of(k)]
        return remote(chunk, chunk, acs.at[w, k % Z], acr.at[w, k % Z], beside)

    def arrived_z(k):
        chunk = wbuf.at[x, c, z_of(k)]
        remote(chunk, chunk, azs.at[k % Z], azr.at[k % Z], over).wait_recv()

    def arrived_x(k):
        chunk = wbuf.at[1 - x, c, z_of(k)]
        remote(chunk, chunk, axs.at[k % Z], axr.at[k % Z], over).wait_recv()

    def arrived_c(w, k):
        chunk = wbuf.at[x if w == 0 else 1 - x, 1 - c, z_of(k)]
        remote(chunk, chunk, acs.at[w, k % Z], acr.at[w, k % Z], beside).wait_recv()

    plus = list(range(1, half + 1))
    minus = [-k for k in range(1, half)]

    def a_forward(k):
        if k >= 0 and k % reach == 0:
            for hop in range(reach, 0, -1):
                if k + hop <= half:
                    send(a_z(k + hop, hop))
        if k <= 0 and (-k) % reach == 0:
            for hop in range(reach, 0, -1):
                if -k + hop <= half - 1:
                    send(a_z(k - hop, -hop))

    def make_chunk():
        loads["master"].wait()
        for q in range(PARTS):
            for r in range(OWN):
                folded[pl.ds((q * OWN + r) * KK, KK), :] = master[pl.ds((r * PARTS + q) * KK, KK), :]
        for k in range(KK):
            wbuf[x, c, z, :, pl.ds(k * 128, 128)] = folded[pl.ds(k, 16, stride=KK), :].astype(BF16)

    def a_start():
        a_forward(0)
        send(a_x(0))
        send(a_c(0, 0))

    def a_got_z(k):
        arrived_z(k)
        a_forward(k)
        send(a_x(k))
        send(a_c(0, k))

    def a_got_x(k):
        arrived_x(k)
        send(a_c(1, k))

    def a_got_c(k):
        arrived_c(0, k)
        arrived_c(1, k)

    def unfold(j):
        pair = lax.rem(z // 2 + (j + Z), half)

        for x_ in range(2):
            outs = [[] for _ in range(PARTS)]
            for side in range(2):
                first = wbuf[x_, 0, 2 * pair + side].astype(F32)
                second = wbuf[x_, 1, 2 * pair + side].astype(F32)
                for h in range(2):
                    a = first[8 * h : 8 * h + 8]
                    b = second[8 * h : 8 * h + 8]
                    outs[2 * h].append(jnp.where(low, a, turn(b)))
                    outs[2 * h + 1].append(jnp.where(low, turn(a), b))
            start = pl.multiple_of(x_ * (8 * Z) + pair * 16, 16)
            for q in range(PARTS):
                wmat[pl.ds(start, 16), pl.ds(q * Q, Q)] = jnp.concatenate(outs[q], 0).astype(BF16)

    def multiply():
        for q in range(PARTS):
            part = lax.dot_general(
                up[:, pl.ds(q * Q, Q)], wmat[:, pl.ds(q * Q, Q)],
                (((1,), (1,)), ((), ())), preferred_element_type=F32,
            )
            if q == 0:
                cg[...] = part
            elif q < PARTS - 1:
                cg[...] += part
            else:
                grad_out[...] = (cg[...] + part).astype(BF16)
        copy = pltpu.make_async_copy(grad_out, grad_hbm, out_sem.at[0])
        copy.start()
        started_out.append(copy)

    started_out = []

    def offset(j):
        return jnp.where(lax.rem(j, 2) == 1, half - (j + 1) // 2, (j // 2) - half)

    order = [half]
    for k in range(half - 1, 0, -1):
        order += [k, -k]
    order.append(0)
    place = {k: j for j, k in enumerate(order)}

    def product():
        loads["ctx"].wait()
        turned = ctx[...].T
        for q in range(PARTS):
            loads[("up", q)].wait()
            gsum[q] = jnp.dot(turned, up[:, pl.ds(q * Q, Q)], preferred_element_type=F32)

    first_core = c == 0

    def fold(w, j):
        z_ = lax.rem(z + (offset(j) + Z), Z)
        x_ = 1 - x if w == 0 else x
        start = pl.multiple_of(x_ * (8 * Z) + z_ * 8, 8)
        s = [gsum[q, pl.ds(start, 8), :] for q in range(PARTS)]
        t = [turn(v) for v in s]
        for h in range(2):
            zero = jnp.where(low, s[2 * h], t[2 * h + 1])
            next_ = jnp.where(low, t[2 * h], s[2 * h + 1])
            own[w, j, pl.ds(8 * h, 8), :] = jnp.where(first_core, zero, next_)
            folded2[h] = jnp.where(first_core, next_, zero)
        csend[w, j] = jnp.concatenate([folded2[0], folded2[1]], 0).astype(BF16)

    folded2 = [None, None]
    pieces = Z // PIECE

    def r_c(w, p):
        part = pl.ds(p * PIECE, PIECE)
        return remote(csend.at[w, part], crecv.at[w, part], rcs.at[w, p], rcr.at[w, p], beside)

    def r_fold(w, p):
        def body(j, carry):
            fold(w, j)
            return carry

        lax.fori_loop(p * PIECE, (p + 1) * PIECE, body, 0)
        send(r_c(w, p))

    def r_x(j):
        return remote(xsend.at[j], xrecv.at[j], rxs.at[j], rxr.at[j], over)

    def r_over(p):
        r_c(0, p).wait_recv()
        for j in range(p * PIECE, (p + 1) * PIECE):
            xsend[j] = (own[0, j] + crecv[0, j].astype(F32)).astype(BF16)
            send(r_x(j))

    def hop_of(k):
        size = abs(k)
        step = (size - 1) % reach + 1
        return step if k > 0 else -step

    def r_z(k):
        return remote(zsend.at[k % Z], zrecv.at[k % Z], rzs.at[k % Z], rzr.at[k % Z], along(hop_of(k)))

    waited = set()

    def feeds(k):
        out = []
        for k_ in plus + minus:
            if k_ - hop_of(k_) == k:
                out.append(k_)
        return out

    def r_sum(k):
        j = place[k]
        p = j // PIECE
        if ("c", p) not in waited:
            waited.add(("c", p))
            r_c(1, p).wait_recv()
        r_x(j).wait_recv()
        total = own[1, j] + crecv[1, j].astype(F32) + xrecv[j].astype(F32)
        for k_ in feeds(k):
            r_z(k_).wait_recv()
            total += zrecv[k_ % Z].astype(F32)
        return total

    def r_send(k):
        zsend[k % Z] = r_sum(k).astype(BF16)
        send(r_z(k))

    def finish():
        total = r_sum(0)
        loads["one"].wait()
        loads["two"].wait()
        scale = 1.0 / math.sqrt(tokens_all)
        for k in range(KK):
            folded[pl.ds(k, 16, stride=KK), :] = total[:, k * 128 : (k + 1) * 128]
        count = jnp.full((KK, 128), step_ref[0] + 1, jnp.int32)
        fix_one = 1.0 - power_of(beta_one, count)
        fix_two = 1.0 - power_of(beta_two, count)
        pair = []
        for b in range(16):
            q, r = b // OWN, b % OWN
            here = pl.ds((r * PARTS + q) * KK, KK)
            gradient = folded[pl.ds(b * KK, KK), :] * scale
            shard = master[here, :]
            first = beta_one * one[here, :] + (1.0 - beta_one) * gradient
            second = beta_two * two[here, :] + (1.0 - beta_two) * gradient * gradient
            update = first / fix_one / (jnp.sqrt(second / fix_two) + adam_eps)
            new = shard - learn_rate * (update + decay_rate * shard)
            one_out[here, :] = first
            two_out[here, :] = second
            stepped[pl.ds(b * KK, KK), :] = new
            pair.append(new)
            if b % 2 == 1:
                sent[pl.ds((b - 1) * KK, 2 * KK), :] = jnp.concatenate(pair, 0).astype(BF16)
                pair = []
        for b in range(bits):
            send(gossip(b))
        for n, (src, dst) in enumerate(((one_out, one_out_hbm), (two_out, two_out_hbm))):
            copy = pltpu.make_async_copy(src, dst, out_sem.at[1 + n])
            copy.start()
            started_out.append(copy)

    def gossip(b):
        return remote(sent, got.at[b], gs.at[b], gr.at[b], partners[b])

    def average():
        for b in range(bits):
            gossip(b).wait_recv()
        chosen = jnp.full((2 * KK, 128), lax.rem(step_ref[0], bits), jnp.int32)
        for n in range(8):
            here = pl.ds(n * 2 * KK, 2 * KK)
            other = got[0, here, :].astype(F32)
            for b in range(1, bits):
                other = jnp.where(chosen == b, got[b, here, :].astype(F32), other)
            mean = 0.5 * (stepped[here, :] + other)
            for s in range(2):
                b = 2 * n + s
                q, r = b // OWN, b % OWN
                master_out[pl.ds((r * PARTS + q) * KK, KK), :] = mean[s * KK : (s + 1) * KK]
        copy = pltpu.make_async_copy(master_out, master_out_hbm, out_sem.at[3])
        copy.start()
        started_out.append(copy)

    make_chunk()
    pl.semaphore_wait(barrier, len(peers))
    a_start()
    product()
    for w in range(2):
        for p in range(pieces):
            r_fold(w, p)

    events = []

    def add(time, what, *args):
        events.append((time, len(events), what, args))

    step_time = 3.6 if reach <= 2 else 5.0
    x_time = 1.0
    z_ready = {0: 2.0}
    for k in plus + minus:
        ready = 2.0 + step_time * (-(-abs(k) // reach)) + 0.1 * abs(k)
        z_ready[k] = ready
        add(ready, a_got_z, k)
    c_ready = {}
    for k in [0] + plus + minus:
        ready = z_ready[k] + 4.5
        add(ready, a_got_x, k)
        c_ready[k] = ready + 2.0
        add(c_ready[k], a_got_c, k) if k else add(c_ready[k], arrived_c, 1, 0)
    add(c_ready[0] - 0.5, arrived_c, 0, 0)
    last = 0.0
    for j in range(half):
        rel = j if j <= half // 2 else j - half
        ks = {(-(2 * rel + d)) % Z for d in (-1, 0, 1)}
        ready = max(c_ready[k] for k in c_ready if k % Z in ks) + 0.2
        last = max(last, ready)
        add(ready, unfold, rel)
    r_ready = {}
    for p in range(pieces):
        add(5.0 + 0.3 * p, r_over, p)
    for k in order:
        ready = 8.0 + x_time * place[k]
        for k_ in feeds(k):
            ready = max(ready, r_ready[k_] + step_time)
        r_ready[k] = ready
        if k:
            add(ready, r_send, k)
    add(r_ready[0], finish)
    add(last + 0.1, multiply)
    add(max(r_ready[0] + 4.0, last + 1.0), average)
    for _, _, what, args in sorted(events, key=lambda e: e[:2]):
        what(*args)
    for copy in started_out:
        copy.wait()
    for copy in started:
        copy.wait_send()


def shards(NG, NF, tokens_all, gossip_step, context, upstream, master, moment_one, moment_two):
    Z = NF // 4
    T, rows = context.shape[1:]
    D = upstream.shape[2]
    flat = master.shape[1]
    Q = D // PARTS
    bits = NG.bit_length() - 1
    DMA = pltpu.SemaphoreType.DMA
    V = pltpu.VMEM
    chunk = (16, Q)
    any_ = pl.BlockSpec(memory_space=pl.ANY)
    shard = jax.ShapeDtypeStruct((flat, 128), F32)
    outs = pl.pallas_call(
        functools.partial(kernel, NG, Z, tokens_all),
        out_shape=(jax.ShapeDtypeStruct((T, rows), BF16), shard, shard, shard),
        in_specs=[pl.BlockSpec(memory_space=pltpu.SMEM)] + [any_] * 5,
        out_specs=(any_,) * 4,
        scratch_shapes=[
            V((T, rows), BF16), V((T, D), BF16), V((flat, 128), F32), V((flat, 128), F32), V((flat, 128), F32),
            V((PARTS, rows, Q), F32), V((2, Z) + chunk, F32), V((2, Z) + chunk, BF16), V((2, Z) + chunk, BF16),
            V((Z,) + chunk, BF16), V((Z,) + chunk, BF16), V((Z,) + chunk, BF16), V((Z,) + chunk, BF16),
            V((2, 2, Z) + chunk, BF16), V((rows, D), BF16), V((T, rows), F32),
            V((flat, 128), F32), V((flat, 128), F32), V((flat, 128), BF16), V((bits, flat, 128), BF16),
            V((T, rows), BF16), V((flat, 128), F32), V((flat, 128), F32), V((flat, 128), F32),
            DMA((4 + PARTS,)), DMA((4,)),
            DMA((Z,)), DMA((Z,)), DMA((Z,)), DMA((Z,)), DMA((2, Z)), DMA((2, Z)),
            DMA((2, Z // PIECE)), DMA((2, Z // PIECE)), DMA((Z,)), DMA((Z,)), DMA((Z,)), DMA((Z,)),
            DMA((bits,)), DMA((bits,)),
        ],
        compiler_params=pltpu.CompilerParams(
            collective_id=0, has_side_effects=True, vmem_limit_bytes=40 * 1024 * 1024
        ),
        name="step",
    )(gossip_step, context[0], upstream[0], master[0], moment_one[0], moment_two[0])
    return tuple(out[None] for out in outs)


def solution(mesh):
    whole = P("group", "fsdp", None)

    def run(gossip_step, context, upstream, master, moment_one, moment_two):
        body = functools.partial(shards, mesh.shape["group"], mesh.shape["fsdp"], context.shape[1])
        return jax.shard_map(
            body, mesh=mesh, in_specs=(P(),) + (whole,) * 5, out_specs=(whole,) * 4, check_vma=False
        )(gossip_step, context, upstream, master, moment_one, moment_two)

    return run
```

```python
import functools
import math

import jax
import jax.numpy as jnp
from jax import lax
from jax.experimental import pallas as pl
from jax.experimental.pallas import tpu as pltpu
from jax.sharding import PartitionSpec as P

MESH = pl.DeviceIdType.MESH
BF16 = jnp.bfloat16
F32 = jnp.float32

beta_one = 0.9
beta_two = 0.999
adam_eps = 1e-08
learn_rate = 0.003
decay_rate = 0.1

OWN = 4
PARTS = 4
REACH = 2
PIECE = 4


def power_of(base, count):
    total = jnp.full(count.shape, 1.0, F32)
    for bit in range(8):
        factor = jnp.float32(base ** (2**bit))
        total = jnp.where(((count >> bit) & 1) == 1, total * factor, total)
    return total


def kernel(
    NG, Z, tokens_all,
    step_ref, ctx_hbm, up_hbm, master_hbm, one_hbm, two_hbm,
    grad_out, master_out, one_out, two_out,
    ctx, up, master, one, two,
    gsum, own, csend, crecv, xsend, xrecv, zsend, zrecv,
    wbuf, wmat, cg, folded, stepped, sent, got,
    in_sem,
    azs, azr, axs, axr, acs, acr,
    rcs, rcr, rxs, rxr, rzs, rzr, gs, gr,
):
    T, D = up.shape
    Q = D // PARTS
    KK = Q // 128
    half = Z // 2
    bits = NG.bit_length() - 1
    group = lax.axis_index("group")
    index = lax.axis_index("fsdp")
    x = index // (2 * Z)
    z = lax.rem(index // 2, Z)
    c = lax.rem(index, 2)

    def at(x_, z_, c_):
        return (group, x_ * (2 * Z) + z_ * 2 + c_)

    def along(k):
        return at(x, lax.rem(z + (k + 2 * Z), Z), c)

    over = at(1 - x, z, c)
    beside = at(x, z, 1 - c)
    partners = [(jnp.bitwise_xor(group, 1 << b), index) for b in range(bits)]

    loads = {}

    def load(name, src, dst, n):
        copy = pltpu.make_async_copy(src, dst, in_sem.at[n])
        copy.start()
        loads[name] = copy

    load("master", master_hbm, master, 0)
    load("ctx", ctx_hbm, ctx, 1)
    for q in range(PARTS):
        load(("up", q), up_hbm.at[:, pl.ds(q * Q, Q)], up.at[:, pl.ds(q * Q, Q)], 2 + q)
    load("one", one_hbm, one, 2 + PARTS)
    load("two", two_hbm, two, 3 + PARTS)

    reach = min(REACH, half)
    hops = sorted({h % Z for h in range(1, reach + 1)} | {-h % Z for h in range(1, reach + 1)})
    peers = [along(h) for h in hops] + [over, beside] + partners
    barrier = pltpu.get_barrier_semaphore()
    for peer in peers:
        pl.semaphore_signal(barrier, inc=1, device_id=peer, device_id_type=MESH)

    started = []

    def send(copy):
        copy.start()
        started.append(copy)

    def remote(src, dst, ss, rs, to):
        return pltpu.make_async_remote_copy(
            src_ref=src, dst_ref=dst, send_sem=ss, recv_sem=rs, device_id=to, device_id_type=MESH
        )

    row8 = lax.broadcasted_iota(jnp.int32, (8, Q), 0)
    low = row8 < OWN

    def turn(value):
        return pltpu.roll(value, 4, 0)

    def z_of(k):
        return lax.rem(z + (2 * Z - k), Z)

    def a_z(k, hop):
        chunk = wbuf.at[x, c, z_of(k - hop)]
        there = k % Z
        return remote(chunk, chunk, azs.at[there], azr.at[there], along(hop))

    def a_x(k):
        chunk = wbuf.at[x, c, z_of(k)]
        return remote(chunk, chunk, axs.at[k % Z], axr.at[k % Z], over)

    def a_c(w, k):
        chunk = wbuf.at[x if w == 0 else 1 - x, c, z_of(k)]
        return remote(chunk, chunk, acs.at[w, k % Z], acr.at[w, k % Z], beside)

    def arrived_z(k):
        chunk = wbuf.at[x, c, z_of(k)]
        remote(chunk, chunk, azs.at[k % Z], azr.at[k % Z], over).wait_recv()

    def arrived_x(k):
        chunk = wbuf.at[1 - x, c, z_of(k)]
        remote(chunk, chunk, axs.at[k % Z], axr.at[k % Z], over).wait_recv()

    def arrived_c(w, k):
        chunk = wbuf.at[x if w == 0 else 1 - x, 1 - c, z_of(k)]
        remote(chunk, chunk, acs.at[w, k % Z], acr.at[w, k % Z], beside).wait_recv()

    plus = list(range(1, half + 1))
    minus = [-k for k in range(1, half)]

    def a_forward(k):
        if k >= 0 and k % reach == 0:
            for hop in range(reach, 0, -1):
                if k + hop <= half:
                    send(a_z(k + hop, hop))
        if k <= 0 and (-k) % reach == 0:
            for hop in range(reach, 0, -1):
                if -k + hop <= half - 1:
                    send(a_z(k - hop, -hop))

    def make_chunk():
        loads["master"].wait()
        for q in range(PARTS):
            for r in range(OWN):
                folded[pl.ds((q * OWN + r) * KK, KK), :] = master[pl.ds((r * PARTS + q) * KK, KK), :]
        for k in range(KK):
            wbuf[x, c, z, :, pl.ds(k * 128, 128)] = folded[pl.ds(k, 16, stride=KK), :].astype(BF16)

    def a_start():
        a_forward(0)
        send(a_x(0))
        send(a_c(0, 0))

    def a_got_z(k):
        arrived_z(k)
        a_forward(k)
        send(a_x(k))
        send(a_c(0, k))

    def a_got_x(k):
        arrived_x(k)
        send(a_c(1, k))

    def a_got_c(k):
        arrived_c(0, k)
        arrived_c(1, k)

    def unfold(j):
        pair = lax.rem(z // 2 + (j + Z), half)

        for x_ in range(2):
            outs = [[] for _ in range(PARTS)]
            for side in range(2):
                first = wbuf[x_, 0, 2 * pair + side].astype(F32)
                second = wbuf[x_, 1, 2 * pair + side].astype(F32)
                for h in range(2):
                    a = first[8 * h : 8 * h + 8]
                    b = second[8 * h : 8 * h + 8]
                    outs[2 * h].append(jnp.where(low, a, turn(b)))
                    outs[2 * h + 1].append(jnp.where(low, turn(a), b))
            start = pl.multiple_of(x_ * (8 * Z) + pair * 16, 16)
            for q in range(PARTS):
                wmat[pl.ds(start, 16), pl.ds(q * Q, Q)] = jnp.concatenate(outs[q], 0).astype(BF16)

    def multiply():
        for q in range(PARTS):
            part = lax.dot_general(
                up[:, pl.ds(q * Q, Q)], wmat[:, pl.ds(q * Q, Q)],
                (((1,), (1,)), ((), ())), preferred_element_type=F32,
            )
            if q == 0:
                cg[...] = part
            elif q < PARTS - 1:
                cg[...] += part
            else:
                grad_out[...] = (cg[...] + part).astype(BF16)

    def offset(j):
        return jnp.where(lax.rem(j, 2) == 1, half - (j + 1) // 2, (j // 2) - half)

    order = [half]
    for k in range(half - 1, 0, -1):
        order += [k, -k]
    order.append(0)
    place = {k: j for j, k in enumerate(order)}

    def product():
        loads["ctx"].wait()
        turned = ctx[...].T
        for q in range(PARTS):
            loads[("up", q)].wait()
            gsum[q] = jnp.dot(turned, up[:, pl.ds(q * Q, Q)], preferred_element_type=F32)

    first_core = c == 0

    def fold(w, j):
        z_ = lax.rem(z + (offset(j) + Z), Z)
        x_ = 1 - x if w == 0 else x
        start = pl.multiple_of(x_ * (8 * Z) + z_ * 8, 8)
        s = [gsum[q, pl.ds(start, 8), :] for q in range(PARTS)]
        t = [turn(v) for v in s]
        for h in range(2):
            zero = jnp.where(low, s[2 * h], t[2 * h + 1])
            next_ = jnp.where(low, t[2 * h], s[2 * h + 1])
            own[w, j, pl.ds(8 * h, 8), :] = jnp.where(first_core, zero, next_)
            folded2[h] = jnp.where(first_core, next_, zero)
        csend[w, j] = jnp.concatenate([folded2[0], folded2[1]], 0).astype(BF16)

    folded2 = [None, None]
    pieces = Z // PIECE

    def r_c(w, p):
        part = pl.ds(p * PIECE, PIECE)
        return remote(csend.at[w, part], crecv.at[w, part], rcs.at[w, p], rcr.at[w, p], beside)

    def r_fold(w, p):
        def body(j, carry):
            fold(w, j)
            return carry

        lax.fori_loop(p * PIECE, (p + 1) * PIECE, body, 0)

    def r_x(j):
        return remote(xsend.at[j], xrecv.at[j], rxs.at[j], rxr.at[j], over)

    def r_over(p):
        r_c(0, p).wait_recv()
        for j in range(p * PIECE, (p + 1) * PIECE):
            xsend[j] = (own[0, j] + crecv[0, j].astype(F32)).astype(BF16)
            send(r_x(j))

    def hop_of(k):
        size = abs(k)
        step = (size - 1) % reach + 1
        return step if k > 0 else -step

    def r_z(k):
        return remote(zsend.at[k % Z], zrecv.at[k % Z], rzs.at[k % Z], rzr.at[k % Z], along(hop_of(k)))

    waited = set()

    def feeds(k):
        out = []
        for k_ in plus + minus:
            if k_ - hop_of(k_) == k:
                out.append(k_)
        return out

    def r_sum(k):
        j = place[k]
        p = j // PIECE
        if ("c", p) not in waited:
            waited.add(("c", p))
            r_c(1, p).wait_recv()
        r_x(j).wait_recv()
        total = own[1, j] + crecv[1, j].astype(F32) + xrecv[j].astype(F32)
        for k_ in feeds(k):
            r_z(k_).wait_recv()
            total += zrecv[k_ % Z].astype(F32)
        return total

    def r_send(k):
        zsend[k % Z] = r_sum(k).astype(BF16)
        send(r_z(k))

    def finish():
        total = r_sum(0)
        loads["one"].wait()
        loads["two"].wait()
        scale = 1.0 / math.sqrt(tokens_all)
        for k in range(KK):
            folded[pl.ds(k, 16, stride=KK), :] = total[:, k * 128 : (k + 1) * 128]
        count = jnp.full((KK, 128), step_ref[0] + 1, jnp.int32)
        fix_one = 1.0 - power_of(beta_one, count)
        fix_two = 1.0 - power_of(beta_two, count)
        pair = []
        for b in range(16):
            q, r = b // OWN, b % OWN
            here = pl.ds((r * PARTS + q) * KK, KK)
            gradient = folded[pl.ds(b * KK, KK), :] * scale
            shard = master[here, :]
            first = beta_one * one[here, :] + (1.0 - beta_one) * gradient
            second = beta_two * two[here, :] + (1.0 - beta_two) * gradient * gradient
            update = first / fix_one / (jnp.sqrt(second / fix_two) + adam_eps)
            new = shard - learn_rate * (update + decay_rate * shard)
            one_out[here, :] = first
            two_out[here, :] = second
            stepped[pl.ds(b * KK, KK), :] = new
            pair.append(new)
            if b % 2 == 1:
                sent[pl.ds((b - 1) * KK, 2 * KK), :] = jnp.concatenate(pair, 0).astype(BF16)
                pair = []
        for b in range(bits):
            send(gossip(b))

    def gossip(b):
        return remote(sent, got.at[b], gs.at[b], gr.at[b], partners[b])

    def average():
        for b in range(bits):
            gossip(b).wait_recv()
        chosen = jnp.full((2 * KK, 128), lax.rem(step_ref[0], bits), jnp.int32)
        for n in range(8):
            here = pl.ds(n * 2 * KK, 2 * KK)
            other = got[0, here, :].astype(F32)
            for b in range(1, bits):
                other = jnp.where(chosen == b, got[b, here, :].astype(F32), other)
            mean = 0.5 * (stepped[here, :] + other)
            for s in range(2):
                b = 2 * n + s
                q, r = b // OWN, b % OWN
                master_out[pl.ds((r * PARTS + q) * KK, KK), :] = mean[s * KK : (s + 1) * KK]

    make_chunk()
    product()
    for w in range(2):
        for p in range(pieces):
            r_fold(w, p)
    pl.semaphore_wait(barrier, len(peers))
    for w in range(2):
        for p in range(pieces):
            send(r_c(w, p))
    a_start()

    events = []

    def add(time, what, *args):
        events.append((time, len(events), what, args))

    step_time = 3.6 if reach <= 2 else 5.0
    x_time = 1.0
    z_ready = {0: 2.0}
    for k in plus + minus:
        ready = 2.0 + step_time * (-(-abs(k) // reach)) + 0.1 * abs(k)
        z_ready[k] = ready
        add(ready, a_got_z, k)
    c_ready = {}
    for k in [0] + plus + minus:
        ready = z_ready[k] + 4.5
        add(ready, a_got_x, k)
        c_ready[k] = ready + 2.0
        add(c_ready[k], a_got_c, k) if k else add(c_ready[k], arrived_c, 1, 0)
    add(c_ready[0] - 0.5, arrived_c, 0, 0)
    last = 0.0
    for j in range(half):
        rel = j if j <= half // 2 else j - half
        ks = {(-(2 * rel + d)) % Z for d in (-1, 0, 1)}
        ready = max(c_ready[k] for k in c_ready if k % Z in ks) + 0.2
        last = max(last, ready)
        add(ready, unfold, rel)
    r_ready = {}
    for p in range(pieces):
        add(5.0 + 0.3 * p, r_over, p)
    for k in order:
        ready = 8.0 + x_time * place[k]
        for k_ in feeds(k):
            ready = max(ready, r_ready[k_] + step_time)
        r_ready[k] = ready
        if k:
            add(ready, r_send, k)
    add(r_ready[0], finish)
    add(last + 0.1, multiply)
    add(max(r_ready[0] + 4.0, last + 1.0), average)
    for _, _, what, args in sorted(events, key=lambda e: e[:2]):
        what(*args)
    for copy in started:
        copy.wait_send()


def store(*refs):
    sems = refs[8]
    copies = [pltpu.make_async_copy(refs[n], refs[4 + n], sems.at[n]) for n in range(4)]
    for copy in copies:
        copy.start()
    for copy in copies:
        copy.wait()


def shards(NG, NF, tokens_all, gossip_step, context, upstream, master, moment_one, moment_two):
    Z = NF // 4
    T, rows = context.shape[1:]
    D = upstream.shape[2]
    flat = master.shape[1]
    Q = D // PARTS
    bits = NG.bit_length() - 1
    DMA = pltpu.SemaphoreType.DMA
    V = pltpu.VMEM
    chunk = (16, Q)
    hbm = pl.BlockSpec(memory_space=pltpu.HBM)
    vmem = pl.BlockSpec(memory_space=pltpu.VMEM)
    outs = pl.pallas_call(
        functools.partial(kernel, NG, Z, tokens_all),
        out_shape=(V((T, rows), BF16), V((flat, 128), F32), V((flat, 128), F32), V((flat, 128), F32)),
        in_specs=[pl.BlockSpec(memory_space=pltpu.SMEM)] + [hbm] * 5,
        out_specs=(vmem,) * 4,
        scratch_shapes=[
            V((T, rows), BF16), V((T, D), BF16), V((flat, 128), F32), V((flat, 128), F32), V((flat, 128), F32),
            V((PARTS, rows, Q), F32), V((2, Z) + chunk, F32), V((2, Z) + chunk, BF16), V((2, Z) + chunk, BF16),
            V((Z,) + chunk, BF16), V((Z,) + chunk, BF16), V((Z,) + chunk, BF16), V((Z,) + chunk, BF16),
            V((2, 2, Z) + chunk, BF16), V((rows, D), BF16), V((T, rows), F32),
            V((flat, 128), F32), V((flat, 128), F32), V((flat, 128), BF16), V((bits, flat, 128), BF16),
            DMA((4 + PARTS,)),
            DMA((Z,)), DMA((Z,)), DMA((Z,)), DMA((Z,)), DMA((2, Z)), DMA((2, Z)),
            DMA((2, Z // PIECE)), DMA((2, Z // PIECE)), DMA((Z,)), DMA((Z,)), DMA((Z,)), DMA((Z,)),
            DMA((bits,)), DMA((bits,)),
        ],
        compiler_params=pltpu.CompilerParams(
            collective_id=0, has_side_effects=True, vmem_limit_bytes=60 * 1024 * 1024
        ),
        name="step",
    )(gossip_step, context[0], upstream[0], master[0], moment_one[0], moment_two[0])
    outs = pl.pallas_call(
        store,
        out_shape=tuple(jax.ShapeDtypeStruct(out.shape, out.dtype) for out in outs),
        in_specs=[vmem] * 4,
        out_specs=(hbm,) * 4,
        scratch_shapes=[DMA((4,))],
        name="store",
    )(*(pltpu.with_memory_space_constraint(out, pltpu.VMEM) for out in outs))
    return tuple(out[None] for out in outs)


def solution(mesh):
    whole = P("group", "fsdp", None)

    def run(gossip_step, context, upstream, master, moment_one, moment_two):
        body = functools.partial(shards, mesh.shape["group"], mesh.shape["fsdp"], context.shape[1])
        return jax.shard_map(
            body, mesh=mesh, in_specs=(P(),) + (whole,) * 5, out_specs=(whole,) * 4, check_vma=False
        )(gossip_step, context, upstream, master, moment_one, moment_two)

    return run
```

```python
import functools
import math

import jax
import jax.numpy as jnp
from jax import lax
from jax.experimental import pallas as pl
from jax.experimental.pallas import tpu as pltpu
from jax.sharding import PartitionSpec as P

MESH = pl.DeviceIdType.MESH
BF16 = jnp.bfloat16
F32 = jnp.float32

beta_one = 0.9
beta_two = 0.999
adam_eps = 1e-08
learn_rate = 0.003
decay_rate = 0.1

OWN = 4
PARTS = 4
WAY_A = {1: 0, 2: 0, 3: 2, 4: 2, 5: 4, 6: 4, 7: 6, 8: 6}
WAY_R = {1: 0, 2: 0, 3: 0, 4: 3, 5: 3, 6: 3, 7: 6, 8: 6}
A_STEP = 2.4
A_HOP = 0.7
A_OVER = 3.5
A_BESIDE = 2.0
A_FIRST = 2.0
A_CROSS = 0.0
A_EACH = 0.0
A_LATE = 18.0
A_LATER = 0.4
R_STEP = 2.4
R_HOP = 0.7
R_FIRST = 6.5
R_CHUNK = 0.6
R_OVER = 3.3
R_PIECE = 0.2
PIECE = 4


def power_of(base, count):
    total = jnp.full(count.shape, 1.0, F32)
    for bit in range(8):
        factor = jnp.float32(base ** (2**bit))
        total = jnp.where(((count >> bit) & 1) == 1, total * factor, total)
    return total


def kernel(
    NG, Z, tokens_all,
    step_ref, ctx_hbm, up_hbm, master_hbm, one_hbm, two_hbm,
    grad_out, master_out, one_out, two_out,
    ctx, up, master, one, two,
    gsum, own, csend, crecv, xsend, xrecv, zsend, zrecv,
    wbuf, wmat, cg, folded, stepped, sent, got,
    in_sem,
    azs, azr, axs, axr, acs, acr,
    rcs, rcr, rxs, rxr, rzs, rzr, gs, gr,
):
    T, D = up.shape
    Q = D // PARTS
    KK = Q // 128
    half = Z // 2
    bits = NG.bit_length() - 1
    group = lax.axis_index("group")
    index = lax.axis_index("fsdp")
    x = index // (2 * Z)
    z = lax.rem(index // 2, Z)
    c = lax.rem(index, 2)

    def at(x_, z_, c_):
        return (group, x_ * (2 * Z) + z_ * 2 + c_)

    def along(k):
        return at(x, lax.rem(z + (k + 2 * Z), Z), c)

    over = at(1 - x, z, c)
    askew = at(1 - x, z, 1 - c)
    beside = at(x, z, 1 - c)
    partners = [(jnp.bitwise_xor(group, 1 << b), index) for b in range(bits)]

    loads = {}

    def load(name, src, dst, n):
        copy = pltpu.make_async_copy(src, dst, in_sem.at[n])
        copy.start()
        loads[name] = copy

    load("master", master_hbm, master, 0)
    load("ctx", ctx_hbm, ctx, 1)
    for q in range(PARTS):
        load(("up", q), up_hbm.at[:, pl.ds(q * Q, Q)], up.at[:, pl.ds(q * Q, Q)], 2 + q)
    load("one", one_hbm, one, 2 + PARTS)
    load("two", two_hbm, two, 3 + PARTS)

    plus = list(range(1, half + 1))
    minus = [-k for k in range(1, half)]

    def before(way, k):
        return way[k] if k > 0 else -way[-k]

    def after(way, k):
        return sorted((n for n in plus + minus if before(way, n) == k), key=lambda n: -abs(n))

    hops = sorted({(k - before(way, k)) % Z for way in (WAY_A, WAY_R) for k in plus + minus})
    peers = [along(h) for h in hops] + [over, askew, beside] + partners
    barrier = pltpu.get_barrier_semaphore()
    for peer in peers:
        pl.semaphore_signal(barrier, inc=1, device_id=peer, device_id_type=MESH)

    started = []

    def send(copy):
        copy.start()
        started.append(copy)

    def remote(src, dst, ss, rs, to):
        return pltpu.make_async_remote_copy(
            src_ref=src, dst_ref=dst, send_sem=ss, recv_sem=rs, device_id=to, device_id_type=MESH
        )

    row8 = lax.broadcasted_iota(jnp.int32, (8, Q), 0)
    low = row8 < OWN

    def turn(value):
        return pltpu.roll(value, 4, 0)

    def z_of(k):
        return lax.rem(z + (2 * Z - k), Z)

    def a_z(k, hop):
        chunk = wbuf.at[x, c, z_of(k - hop)]
        there = k % Z
        return remote(chunk, chunk, azs.at[there], azr.at[there], along(hop))

    def skew(k):
        return k % 2 == 1

    def a_x(k):
        chunk = wbuf.at[x, c, z_of(k)]
        return remote(chunk, chunk, axs.at[k % Z], axr.at[k % Z], askew if skew(k) else over)

    def over_chunk(k):
        return wbuf.at[1 - x, 1 - c if skew(k) else c, z_of(k)]

    def a_c(w, k):
        chunk = wbuf.at[x, c, z_of(k)] if w == 0 else over_chunk(k)
        return remote(chunk, chunk, acs.at[w, k % Z], acr.at[w, k % Z], beside)

    def arrived_z(k):
        chunk = wbuf.at[x, c, z_of(k)]
        remote(chunk, chunk, azs.at[k % Z], azr.at[k % Z], over).wait_recv()

    def arrived_x(k):
        chunk = over_chunk(k)
        remote(chunk, chunk, axs.at[k % Z], axr.at[k % Z], over).wait_recv()

    def arrived_c(w, k):
        chunk = wbuf.at[x, 1 - c, z_of(k)] if w == 0 else wbuf.at[1 - x, c if skew(k) else 1 - c, z_of(k)]
        remote(chunk, chunk, acs.at[w, k % Z], acr.at[w, k % Z], beside).wait_recv()

    def a_forward(k):
        for n in after(WAY_A, k):
            send(a_z(n, n - k))

    def make_chunk():
        loads["master"].wait()
        for q in range(PARTS):
            for r in range(OWN):
                folded[pl.ds((q * OWN + r) * KK, KK), :] = master[pl.ds((r * PARTS + q) * KK, KK), :]
        for k in range(KK):
            wbuf[x, c, z, :, pl.ds(k * 128, 128)] = folded[pl.ds(k, 16, stride=KK), :].astype(BF16)

    def a_start():
        a_forward(0)
        send(a_c(0, 0))

    def a_got_z(k):
        arrived_z(k)
        a_forward(k)
        send(a_c(0, k))

    def a_cross(k):
        send(a_x(k))

    def a_got_x(k):
        arrived_x(k)
        send(a_c(1, k))

    def a_got_c(k):
        arrived_c(0, k)
        arrived_c(1, k)

    def unfold(j):
        pair = lax.rem(z // 2 + (j + Z), half)

        for x_ in range(2):
            outs = [[] for _ in range(PARTS)]
            for side in range(2):
                first = wbuf[x_, 0, 2 * pair + side].astype(F32)
                second = wbuf[x_, 1, 2 * pair + side].astype(F32)
                for h in range(2):
                    a = first[8 * h : 8 * h + 8]
                    b = second[8 * h : 8 * h + 8]
                    outs[2 * h].append(jnp.where(low, a, turn(b)))
                    outs[2 * h + 1].append(jnp.where(low, turn(a), b))
            start = pl.multiple_of(x_ * (8 * Z) + pair * 16, 16)
            for q in range(PARTS):
                wmat[pl.ds(start, 16), pl.ds(q * Q, Q)] = jnp.concatenate(outs[q], 0).astype(BF16)

    def multiply():
        for q in range(PARTS):
            part = lax.dot_general(
                up[:, pl.ds(q * Q, Q)], wmat[:, pl.ds(q * Q, Q)],
                (((1,), (1,)), ((), ())), preferred_element_type=F32,
            )
            if q == 0:
                cg[...] = part
            elif q < PARTS - 1:
                cg[...] += part
            else:
                grad_out[...] = (cg[...] + part).astype(BF16)

    def offset(j):
        return jnp.where(lax.rem(j, 2) == 1, half - (j + 1) // 2, (j // 2) - half)

    order = [half]
    for k in range(half - 1, 0, -1):
        order += [k, -k]
    order.append(0)
    place = {k: j for j, k in enumerate(order)}

    def product():
        loads["ctx"].wait()
        turned = ctx[...].T
        for q in range(PARTS):
            loads[("up", q)].wait()
            gsum[q] = jnp.dot(turned, up[:, pl.ds(q * Q, Q)], preferred_element_type=F32)

    def fold(w, j):
        first_core = lax.rem(c + j, 2) == 0 if w == 0 else c == 0
        z_ = lax.rem(z + (offset(j) + Z), Z)
        x_ = 1 - x if w == 0 else x
        start = pl.multiple_of(x_ * (8 * Z) + z_ * 8, 8)
        s = [gsum[q, pl.ds(start, 8), :] for q in range(PARTS)]
        t = [turn(v) for v in s]
        for h in range(2):
            zero = jnp.where(low, s[2 * h], t[2 * h + 1])
            next_ = jnp.where(low, t[2 * h], s[2 * h + 1])
            own[w, j, pl.ds(8 * h, 8), :] = jnp.where(first_core, zero, next_)
            folded2[h] = jnp.where(first_core, next_, zero)
        csend[w, j] = jnp.concatenate([folded2[0], folded2[1]], 0).astype(BF16)

    folded2 = [None, None]
    pieces = Z // PIECE

    def r_c(w, p):
        part = pl.ds(p * PIECE, PIECE)
        return remote(csend.at[w, part], crecv.at[w, part], rcs.at[w, p], rcr.at[w, p], beside)

    def r_fold(w, p):
        def body(j, carry):
            fold(w, j)
            return carry

        lax.fori_loop(p * PIECE, (p + 1) * PIECE, body, 0)

    def r_x(j):
        return remote(xsend.at[j], xrecv.at[j], rxs.at[j], rxr.at[j], askew if j % 2 else over)

    def r_over(p):
        r_c(0, p).wait_recv()
        for j in range(p * PIECE, (p + 1) * PIECE):
            xsend[j] = (own[0, j] + crecv[0, j].astype(F32)).astype(BF16)
            send(r_x(j))

    def hop_of(k):
        return k - before(WAY_R, k)

    def r_z(k):
        return remote(zsend.at[k % Z], zrecv.at[k % Z], rzs.at[k % Z], rzr.at[k % Z], along(hop_of(k)))

    waited = set()

    def r_sum(k):
        j = place[k]
        p = j // PIECE
        if ("c", p) not in waited:
            waited.add(("c", p))
            r_c(1, p).wait_recv()
        r_x(j).wait_recv()
        total = own[1, j] + crecv[1, j].astype(F32) + xrecv[j].astype(F32)
        for k_ in after(WAY_R, k):
            r_z(k_).wait_recv()
            total += zrecv[k_ % Z].astype(F32)
        return total

    def r_send(k):
        zsend[k % Z] = r_sum(k).astype(BF16)
        send(r_z(k))

    def finish():
        total = r_sum(0)
        loads["one"].wait()
        loads["two"].wait()
        scale = 1.0 / math.sqrt(tokens_all)
        for k in range(KK):
            folded[pl.ds(k, 16, stride=KK), :] = total[:, k * 128 : (k + 1) * 128]
        count = jnp.full((KK, 128), step_ref[0] + 1, jnp.int32)
        fix_one = 1.0 - power_of(beta_one, count)
        fix_two = 1.0 - power_of(beta_two, count)
        pair = []
        for b in range(16):
            q, r = b // OWN, b % OWN
            here = pl.ds((r * PARTS + q) * KK, KK)
            gradient = folded[pl.ds(b * KK, KK), :] * scale
            shard = master[here, :]
            first = beta_one * one[here, :] + (1.0 - beta_one) * gradient
            second = beta_two * two[here, :] + (1.0 - beta_two) * gradient * gradient
            update = first / fix_one / (jnp.sqrt(second / fix_two) + adam_eps)
            new = shard - learn_rate * (update + decay_rate * shard)
            one_out[here, :] = first
            two_out[here, :] = second
            stepped[pl.ds(b * KK, KK), :] = new
            pair.append(new)
            if b % 2 == 1:
                sent[pl.ds((b - 1) * KK, 2 * KK), :] = jnp.concatenate(pair, 0).astype(BF16)
                pair = []
        for b in range(bits):
            send(gossip(b))

    def gossip(b):
        return remote(sent, got.at[b], gs.at[b], gr.at[b], partners[b])

    def average():
        for b in range(bits):
            gossip(b).wait_recv()
        chosen = jnp.full((2 * KK, 128), lax.rem(step_ref[0], bits), jnp.int32)
        for n in range(8):
            here = pl.ds(n * 2 * KK, 2 * KK)
            other = got[0, here, :].astype(F32)
            for b in range(1, bits):
                other = jnp.where(chosen == b, got[b, here, :].astype(F32), other)
            mean = 0.5 * (stepped[here, :] + other)
            for s in range(2):
                b = 2 * n + s
                q, r = b // OWN, b % OWN
                master_out[pl.ds((r * PARTS + q) * KK, KK), :] = mean[s * KK : (s + 1) * KK]

    make_chunk()
    product()
    for w in range(2):
        for p in range(pieces):
            r_fold(w, p)
    pl.semaphore_wait(barrier, len(peers))
    for w in range(2):
        for p in range(pieces):
            send(r_c(w, p))
    a_start()

    events = []

    def add(time, what, *args):
        events.append((time, len(events), what, args))

    z_ready = {0: A_FIRST}
    for k in plus + minus:
        z_ready[k] = z_ready[before(WAY_A, k)] + A_STEP + A_HOP * abs(k - before(WAY_A, k))
        add(z_ready[k], a_got_z, k)
    c_ready = {}
    for i, k in enumerate([0] + [k for pair in zip(plus, minus + [None]) for k in pair if k is not None]):
        cross = max(z_ready[k] + 0.01, A_CROSS + A_EACH * i)
        add(cross, a_cross, k)
        ready = max(cross + A_OVER, A_LATE + A_LATER * i)
        add(ready, a_got_x, k)
        c_ready[k] = ready + A_BESIDE
        add(c_ready[k], a_got_c, k)
    last = 0.0
    for j in range(half):
        rel = j if j <= half // 2 else j - half
        ks = {(-(2 * rel + d)) % Z for d in (-1, 0, 1)}
        ready = max(c_ready[k] for k in c_ready if k % Z in ks) + 0.2
        last = max(last, ready)
        add(ready, unfold, rel)
    r_ready = {}
    for p in range(pieces):
        add(R_OVER + R_PIECE * p, r_over, p)
    for k in order:
        ready = R_FIRST + R_CHUNK * place[k]
        for k_ in after(WAY_R, k):
            ready = max(ready, r_ready[k_] + R_STEP + R_HOP * abs(hop_of(k_)))
        r_ready[k] = ready
        if k:
            add(ready, r_send, k)
    add(r_ready[0], finish)
    add(last + 0.1, multiply)
    add(max(r_ready[0] + 4.0, last + 1.0), average)
    for _, _, what, args in sorted(events, key=lambda e: e[:2]):
        what(*args)
    for copy in started:
        copy.wait_send()


def store(*refs):
    sems = refs[8]
    copies = [pltpu.make_async_copy(refs[n], refs[4 + n], sems.at[n]) for n in range(4)]
    for copy in copies:
        copy.start()
    for copy in copies:
        copy.wait()


def shards(NG, NF, tokens_all, gossip_step, context, upstream, master, moment_one, moment_two):
    Z = NF // 4
    T, rows = context.shape[1:]
    D = upstream.shape[2]
    flat = master.shape[1]
    Q = D // PARTS
    bits = NG.bit_length() - 1
    DMA = pltpu.SemaphoreType.DMA
    V = pltpu.VMEM
    chunk = (16, Q)
    hbm = pl.BlockSpec(memory_space=pltpu.HBM)
    vmem = pl.BlockSpec(memory_space=pltpu.VMEM)
    outs = pl.pallas_call(
        functools.partial(kernel, NG, Z, tokens_all),
        out_shape=(V((T, rows), BF16), V((flat, 128), F32), V((flat, 128), F32), V((flat, 128), F32)),
        in_specs=[pl.BlockSpec(memory_space=pltpu.SMEM)] + [hbm] * 5,
        out_specs=(vmem,) * 4,
        scratch_shapes=[
            V((T, rows), BF16), V((T, D), BF16), V((flat, 128), F32), V((flat, 128), F32), V((flat, 128), F32),
            V((PARTS, rows, Q), F32), V((2, Z) + chunk, F32), V((2, Z) + chunk, BF16), V((2, Z) + chunk, BF16),
            V((Z,) + chunk, BF16), V((Z,) + chunk, BF16), V((Z,) + chunk, BF16), V((Z,) + chunk, BF16),
            V((2, 2, Z) + chunk, BF16), V((rows, D), BF16), V((T, rows), F32),
            V((flat, 128), F32), V((flat, 128), F32), V((flat, 128), BF16), V((bits, flat, 128), BF16),
            DMA((4 + PARTS,)),
            DMA((Z,)), DMA((Z,)), DMA((Z,)), DMA((Z,)), DMA((2, Z)), DMA((2, Z)),
            DMA((2, Z // PIECE)), DMA((2, Z // PIECE)), DMA((Z,)), DMA((Z,)), DMA((Z,)), DMA((Z,)),
            DMA((bits,)), DMA((bits,)),
        ],
        compiler_params=pltpu.CompilerParams(
            collective_id=0, has_side_effects=True, vmem_limit_bytes=60 * 1024 * 1024
        ),
        name="step",
    )(gossip_step, context[0], upstream[0], master[0], moment_one[0], moment_two[0])
    outs = pl.pallas_call(
        store,
        out_shape=tuple(jax.ShapeDtypeStruct(out.shape, out.dtype) for out in outs),
        in_specs=[vmem] * 4,
        out_specs=(hbm,) * 4,
        scratch_shapes=[DMA((4,))],
        name="store",
    )(*(pltpu.with_memory_space_constraint(out, pltpu.VMEM) for out in outs))
    return tuple(out[None] for out in outs)


def solution(mesh):
    whole = P("group", "fsdp", None)

    def run(gossip_step, context, upstream, master, moment_one, moment_two):
        body = functools.partial(shards, mesh.shape["group"], mesh.shape["fsdp"], context.shape[1])
        return jax.shard_map(
            body, mesh=mesh, in_specs=(P(),) + (whole,) * 5, out_specs=(whole,) * 4, check_vma=False
        )(gossip_step, context, upstream, master, moment_one, moment_two)

    return run
```

```python
import functools
import math

import jax
import jax.numpy as jnp
from jax import lax
from jax.experimental import pallas as pl
from jax.experimental.pallas import tpu as pltpu
from jax.sharding import PartitionSpec as P

MESH = pl.DeviceIdType.MESH
BF16 = jnp.bfloat16
F32 = jnp.float32

beta_one = 0.9
beta_two = 0.999
adam_eps = 1e-08
learn_rate = 0.003
decay_rate = 0.1

OWN = 4
PARTS = 4
WAY_A = {1: 0, 2: 0, 3: 2, 4: 2, 5: 4, 6: 4, 7: 6, 8: 6}
WAY_R = {1: 0, 2: 0, 3: 0, 4: 3, 5: 3, 6: 3, 7: 6, 8: 6}
A_STEP = 2.4
A_HOP = 0.7
A_OVER = 3.5
A_BESIDE = 2.0
A_FIRST = 2.0
A_CROSS = 0.0
A_EACH = 0.0
A_LATE = 18.0
A_LATER = 0.4
R_STEP = 2.4
R_HOP = 0.7
R_FIRST = 7.5
R_CHUNK = 0.6
R_OVER = 3.3
R_PIECE = 0.2
PIECE = 4


def power_of(base, count):
    total = jnp.full(count.shape, 1.0, F32)
    for bit in range(8):
        factor = jnp.float32(base ** (2**bit))
        total = jnp.where(((count >> bit) & 1) == 1, total * factor, total)
    return total


def kernel(
    NG, Z, tokens_all,
    step_ref, ctx_hbm, up_hbm, master_hbm, one_hbm, two_hbm,
    grad_out, master_out, one_out, two_out,
    ctx, up, master, one, two,
    gsum, own, csend, crecv, xsend, xrecv, zsend, zrecv,
    wbuf, wmat, folded, stepped, sent, got,
    in_sem,
    azs, azr, axs, axr, acs, acr,
    rcs, rcr, rxs, rxr, rzs, rzr, gs, gr,
):
    T, D = up.shape
    Q = D // PARTS
    KK = Q // 128
    half = Z // 2
    bits = NG.bit_length() - 1
    group = lax.axis_index("group")
    index = lax.axis_index("fsdp")
    x = index // (2 * Z)
    z = lax.rem(index // 2, Z)
    c = lax.rem(index, 2)

    def at(x_, z_, c_):
        return (group, x_ * (2 * Z) + z_ * 2 + c_)

    def along(k, core=None):
        return at(x, lax.rem(z + (k + 2 * Z), Z), c if core is None else core)

    over = at(1 - x, z, c)
    askew = at(1 - x, z, 1 - c)
    beside = at(x, z, 1 - c)
    partners = [(jnp.bitwise_xor(group, 1 << b), index) for b in range(bits)]

    loads = {}

    def load(name, src, dst, n):
        copy = pltpu.make_async_copy(src, dst, in_sem.at[n])
        copy.start()
        loads[name] = copy

    load("master", master_hbm, master, 0)
    load("ctx", ctx_hbm, ctx, 1)
    for q in range(PARTS):
        load(("up", q), up_hbm.at[:, pl.ds(q * Q, Q)], up.at[:, pl.ds(q * Q, Q)], 2 + q)
    load("one", one_hbm, one, 2 + PARTS)
    load("two", two_hbm, two, 3 + PARTS)

    plus = list(range(1, half + 1))
    minus = [-k for k in range(1, half)]

    def before(way, k):
        return way[k] if k > 0 else -way[-k]

    def after(way, k):
        return sorted((n for n in plus + minus if before(way, n) == k), key=lambda n: -abs(n))

    def hops(way):
        return sorted({(k - before(way, k)) % Z for k in plus + minus})

    def steps(k):
        return 0 if k == 0 else 1 + steps(before(WAY_R, k))

    peers = [along(h) for h in hops(WAY_A)] + [along(h, 1 - c) for h in hops(WAY_R)] + [over, askew, beside] + partners
    barrier = pltpu.get_barrier_semaphore()
    for peer in peers:
        pl.semaphore_signal(barrier, inc=1, device_id=peer, device_id_type=MESH)

    started = []

    def send(copy):
        copy.start()
        started.append(copy)

    def remote(src, dst, ss, rs, to):
        return pltpu.make_async_remote_copy(
            src_ref=src, dst_ref=dst, send_sem=ss, recv_sem=rs, device_id=to, device_id_type=MESH
        )

    row8 = lax.broadcasted_iota(jnp.int32, (8, Q), 0)
    low = row8 < OWN

    def turn(value):
        return pltpu.roll(value, 4, 0)

    def z_of(k):
        return lax.rem(z + (2 * Z - k), Z)

    def a_z(k, hop):
        chunk = wbuf.at[x, c, z_of(k - hop)]
        there = k % Z
        return remote(chunk, chunk, azs.at[there], azr.at[there], along(hop))

    def skew(k):
        return k % 2 == 1

    def a_x(k):
        chunk = wbuf.at[x, c, z_of(k)]
        return remote(chunk, chunk, axs.at[k % Z], axr.at[k % Z], askew if skew(k) else over)

    def over_chunk(k):
        return wbuf.at[1 - x, 1 - c if skew(k) else c, z_of(k)]

    def a_c(w, k):
        chunk = wbuf.at[x, c, z_of(k)] if w == 0 else over_chunk(k)
        return remote(chunk, chunk, acs.at[w, k % Z], acr.at[w, k % Z], beside)

    def arrived_z(k):
        chunk = wbuf.at[x, c, z_of(k)]
        remote(chunk, chunk, azs.at[k % Z], azr.at[k % Z], over).wait_recv()

    def arrived_x(k):
        chunk = over_chunk(k)
        remote(chunk, chunk, axs.at[k % Z], axr.at[k % Z], over).wait_recv()

    def arrived_c(w, k):
        chunk = wbuf.at[x, 1 - c, z_of(k)] if w == 0 else wbuf.at[1 - x, c if skew(k) else 1 - c, z_of(k)]
        remote(chunk, chunk, acs.at[w, k % Z], acr.at[w, k % Z], beside).wait_recv()

    def a_forward(k):
        for n in after(WAY_A, k):
            send(a_z(n, n - k))

    def make_chunk():
        loads["master"].wait()
        for q in range(PARTS):
            for r in range(OWN):
                folded[pl.ds((q * OWN + r) * KK, KK), :] = master[pl.ds((r * PARTS + q) * KK, KK), :]
        for k in range(KK):
            wbuf[x, c, z, :, pl.ds(k * 128, 128)] = folded[pl.ds(k, 16, stride=KK), :].astype(BF16)

    def a_start():
        a_forward(0)
        send(a_c(0, 0))

    def a_got_z(k):
        arrived_z(k)
        a_forward(k)
        send(a_c(0, k))

    def a_cross(k):
        send(a_x(k))

    def a_got_x(k):
        arrived_x(k)
        send(a_c(1, k))

    def a_got_c(k):
        arrived_c(0, k)
        arrived_c(1, k)

    def unfold(j):
        pair = lax.rem(z // 2 + (j + Z), half)

        for x_ in range(2):
            outs = [[] for _ in range(PARTS)]
            for side in range(2):
                first = wbuf[x_, 0, 2 * pair + side].astype(F32)
                second = wbuf[x_, 1, 2 * pair + side].astype(F32)
                for h in range(2):
                    a = first[8 * h : 8 * h + 8]
                    b = second[8 * h : 8 * h + 8]
                    outs[2 * h].append(jnp.where(low, a, turn(b)))
                    outs[2 * h + 1].append(jnp.where(low, turn(a), b))
            start = pl.multiple_of(x_ * (8 * Z) + pair * 16, 16)
            for q in range(PARTS):
                wmat[pl.ds(start, 16), pl.ds(q * Q, Q)] = jnp.concatenate(outs[q], 0).astype(BF16)

    def multiply():
        total = lax.dot_general(up[...], wmat[...], (((1,), (1,)), ((), ())), preferred_element_type=F32)
        grad_out[...] = total.astype(BF16)

    order = [half]
    for k in range(half - 1, 0, -1):
        order += [k, -k]
    order.append(0)
    place = {k: j for j, k in enumerate(order)}

    def product():
        loads["ctx"].wait()
        turned = ctx[...].T
        for q in range(PARTS):
            loads[("up", q)].wait()
            gsum[q] = jnp.dot(turned, up[:, pl.ds(q * Q, Q)], preferred_element_type=F32)

    def fold(w, j):
        turns = steps(order[j]) + (j if w == 0 else 0)
        first_core = c == turns % 2
        z_ = lax.rem(z + (order[j] + Z), Z)
        x_ = 1 - x if w == 0 else x
        start = pl.multiple_of(x_ * (8 * Z) + z_ * 8, 8)
        s = [gsum[q, pl.ds(start, 8), :] for q in range(PARTS)]
        t = [turn(v) for v in s]
        for h in range(2):
            zero = jnp.where(low, s[2 * h], t[2 * h + 1])
            next_ = jnp.where(low, t[2 * h], s[2 * h + 1])
            own[w, j, pl.ds(8 * h, 8), :] = jnp.where(first_core, zero, next_)
            folded2[h] = jnp.where(first_core, next_, zero)
        csend[w, j] = jnp.concatenate([folded2[0], folded2[1]], 0).astype(BF16)

    folded2 = [None, None]
    pieces = Z // PIECE

    def r_c(w, p):
        part = pl.ds(p * PIECE, PIECE)
        return remote(csend.at[w, part], crecv.at[w, part], rcs.at[w, p], rcr.at[w, p], beside)

    def r_fold(w, p):
        for j in range(p * PIECE, (p + 1) * PIECE):
            fold(w, j)

    def r_x(j):
        return remote(xsend.at[j], xrecv.at[j], rxs.at[j], rxr.at[j], askew if j % 2 else over)

    def r_over(p):
        r_c(0, p).wait_recv()
        for j in range(p * PIECE, (p + 1) * PIECE):
            xsend[j] = (own[0, j] + crecv[0, j].astype(F32)).astype(BF16)
            send(r_x(j))

    def hop_of(k):
        return k - before(WAY_R, k)

    def r_z(k):
        return remote(zsend.at[k % Z], zrecv.at[k % Z], rzs.at[k % Z], rzr.at[k % Z], along(hop_of(k), 1 - c))

    waited = set()

    def r_sum(k):
        j = place[k]
        p = j // PIECE
        if ("c", p) not in waited:
            waited.add(("c", p))
            r_c(1, p).wait_recv()
        r_x(j).wait_recv()
        total = own[1, j] + crecv[1, j].astype(F32) + xrecv[j].astype(F32)
        for k_ in after(WAY_R, k):
            r_z(k_).wait_recv()
            total += zrecv[k_ % Z].astype(F32)
        return total

    def r_send(k):
        zsend[k % Z] = r_sum(k).astype(BF16)
        send(r_z(k))

    def finish():
        total = r_sum(0)
        loads["one"].wait()
        loads["two"].wait()
        scale = 1.0 / math.sqrt(tokens_all)
        for k in range(KK):
            folded[pl.ds(k, 16, stride=KK), :] = total[:, k * 128 : (k + 1) * 128]
        count = jnp.full((KK, 128), step_ref[0] + 1, jnp.int32)
        fix_one = 1.0 - power_of(beta_one, count)
        fix_two = 1.0 - power_of(beta_two, count)
        pair = []
        for b in range(16):
            q, r = b // OWN, b % OWN
            here = pl.ds((r * PARTS + q) * KK, KK)
            gradient = folded[pl.ds(b * KK, KK), :] * scale
            shard = master[here, :]
            first = beta_one * one[here, :] + (1.0 - beta_one) * gradient
            second = beta_two * two[here, :] + (1.0 - beta_two) * gradient * gradient
            update = first / fix_one / (jnp.sqrt(second / fix_two) + adam_eps)
            new = shard - learn_rate * (update + decay_rate * shard)
            one_out[here, :] = first
            two_out[here, :] = second
            stepped[pl.ds(b * KK, KK), :] = new
            pair.append(new)
            if b % 2 == 1:
                sent[pl.ds((b - 1) * KK, 2 * KK), :] = jnp.concatenate(pair, 0).astype(BF16)
                pair = []
        for b in range(bits):
            send(gossip(b))

    def gossip(b):
        return remote(sent, got.at[b], gs.at[b], gr.at[b], partners[b])

    def average():
        for b in range(bits):
            gossip(b).wait_recv()
        chosen = jnp.full((2 * KK, 128), lax.rem(step_ref[0], bits), jnp.int32)
        for n in range(8):
            here = pl.ds(n * 2 * KK, 2 * KK)
            other = got[0, here, :].astype(F32)
            for b in range(1, bits):
                other = jnp.where(chosen == b, got[b, here, :].astype(F32), other)
            mean = 0.5 * (stepped[here, :] + other)
            for s in range(2):
                b = 2 * n + s
                q, r = b // OWN, b % OWN
                master_out[pl.ds((r * PARTS + q) * KK, KK), :] = mean[s * KK : (s + 1) * KK]

    make_chunk()
    product()
    pl.semaphore_wait(barrier, len(peers))
    a_start()
    for w in range(2):
        for p in range(pieces):
            r_fold(w, p)
            send(r_c(w, p))

    events = []

    def add(time, what, *args):
        events.append((time, len(events), what, args))

    z_ready = {0: A_FIRST}
    for k in plus + minus:
        z_ready[k] = z_ready[before(WAY_A, k)] + A_STEP + A_HOP * abs(k - before(WAY_A, k))
        add(z_ready[k], a_got_z, k)
    c_ready = {}
    for i, k in enumerate([0] + [k for pair in zip(plus, minus + [None]) for k in pair if k is not None]):
        cross = max(z_ready[k] + 0.01, A_CROSS + A_EACH * i)
        add(cross, a_cross, k)
        ready = max(cross + A_OVER, A_LATE + A_LATER * i)
        add(ready, a_got_x, k)
        c_ready[k] = ready + A_BESIDE
        add(c_ready[k], a_got_c, k)
    last = 0.0
    for j in range(half):
        rel = j if j <= half // 2 else j - half
        ks = {(-(2 * rel + d)) % Z for d in (-1, 0, 1)}
        ready = max(c_ready[k] for k in c_ready if k % Z in ks) + 0.2
        last = max(last, ready)
        add(ready, unfold, rel)
    r_ready = {}
    for p in range(pieces):
        add(R_OVER + R_PIECE * p, r_over, p)
    for k in order:
        ready = R_FIRST + R_CHUNK * place[k]
        for k_ in after(WAY_R, k):
            ready = max(ready, r_ready[k_] + R_STEP + R_HOP * abs(hop_of(k_)))
        r_ready[k] = ready
        if k:
            add(ready, r_send, k)
    add(r_ready[0], finish)
    add(last + 0.1, multiply)
    add(max(r_ready[0] + 4.0, last + 1.0), average)
    for _, _, what, args in sorted(events, key=lambda e: e[:2]):
        what(*args)
    for copy in started:
        copy.wait_send()


def store(*refs):
    sems = refs[8]
    copies = [pltpu.make_async_copy(refs[n], refs[4 + n], sems.at[n]) for n in range(4)]
    for copy in copies:
        copy.start()
    for copy in copies:
        copy.wait()


def shards(NG, NF, tokens_all, gossip_step, context, upstream, master, moment_one, moment_two):
    Z = NF // 4
    T, rows = context.shape[1:]
    D = upstream.shape[2]
    flat = master.shape[1]
    Q = D // PARTS
    bits = NG.bit_length() - 1
    DMA = pltpu.SemaphoreType.DMA
    V = pltpu.VMEM
    chunk = (16, Q)
    hbm = pl.BlockSpec(memory_space=pltpu.HBM)
    vmem = pl.BlockSpec(memory_space=pltpu.VMEM)
    outs = pl.pallas_call(
        functools.partial(kernel, NG, Z, tokens_all),
        out_shape=(V((T, rows), BF16), V((flat, 128), F32), V((flat, 128), F32), V((flat, 128), F32)),
        in_specs=[pl.BlockSpec(memory_space=pltpu.SMEM)] + [hbm] * 5,
        out_specs=(vmem,) * 4,
        scratch_shapes=[
            V((T, rows), BF16), V((T, D), BF16), V((flat, 128), F32), V((flat, 128), F32), V((flat, 128), F32),
            V((PARTS, rows, Q), F32), V((2, Z) + chunk, F32), V((2, Z) + chunk, BF16), V((2, Z) + chunk, BF16),
            V((Z,) + chunk, BF16), V((Z,) + chunk, BF16), V((Z,) + chunk, BF16), V((Z,) + chunk, BF16),
            V((2, 2, Z) + chunk, BF16), V((rows, D), BF16),
            V((flat, 128), F32), V((flat, 128), F32), V((flat, 128), BF16), V((bits, flat, 128), BF16),
            DMA((4 + PARTS,)),
            DMA((Z,)), DMA((Z,)), DMA((Z,)), DMA((Z,)), DMA((2, Z)), DMA((2, Z)),
            DMA((2, Z // PIECE)), DMA((2, Z // PIECE)), DMA((Z,)), DMA((Z,)), DMA((Z,)), DMA((Z,)),
            DMA((bits,)), DMA((bits,)),
        ],
        compiler_params=pltpu.CompilerParams(
            collective_id=0, has_side_effects=True, vmem_limit_bytes=60 * 1024 * 1024
        ),
        name="step",
    )(gossip_step, context[0], upstream[0], master[0], moment_one[0], moment_two[0])
    outs = pl.pallas_call(
        store,
        out_shape=tuple(jax.ShapeDtypeStruct(out.shape, out.dtype) for out in outs),
        in_specs=[vmem] * 4,
        out_specs=(hbm,) * 4,
        scratch_shapes=[DMA((4,))],
        name="store",
    )(*(pltpu.with_memory_space_constraint(out, pltpu.VMEM) for out in outs))
    return tuple(out[None] for out in outs)


def solution(mesh):
    whole = P("group", "fsdp", None)

    def run(gossip_step, context, upstream, master, moment_one, moment_two):
        body = functools.partial(shards, mesh.shape["group"], mesh.shape["fsdp"], context.shape[1])
        return jax.shard_map(
            body, mesh=mesh, in_specs=(P(),) + (whole,) * 5, out_specs=(whole,) * 4, check_vma=False
        )(gossip_step, context, upstream, master, moment_one, moment_two)

    return run
```
